32 devices in a mesh: gx: 16 (over z, x, core), gz: 2 (over y).
Axes of the slice: x: 2, y: 2, z: 4, core: 2. Of those that a mesh axis runs over, the one named last changes fastest.
Arguments:
- right_side: float32 [3, 6, 128, 1024], P(None, 'gz', 'gx'), may hold values from -48 to 48
- density: float32 [6, 128, 1024], P('gz', 'gx'), may hold values from 0.5 to 4
Outputs:
- solution_field: float32 [3, 6, 128, 1024], P(None, 'gz', 'gx')
The draws below stay inside these ranges and needn't reach their ends.
All inputs are finite; a program needn't handle non-finite values.
Results may differ from the reference program's by a relative error of at most 0.0001.
Values sent between devices are 32-bit elements; how exact they have to be, the bound alone decides.
A program may use at most 128 MiB of HBM per device.

```python
import math
import jax
import jax.numpy as jnp
from jax import lax

COMPONENTS = 3
NY = 1024
LEVELS = 4
PRE = 2
POST = 2
COARSE_SWEEPS = 3
CYCLES = 2
NX = 128
NZ = 6


def draw_right_side(key, part):
    first_key = jax.random.fold_in(key, 0)
    shape = (COMPONENTS, NZ, NX, NY)
    return jnp.clip(8.0 * jax.random.normal(first_key, shape, jnp.float32), -48.0, 48.0)


def level_of(own_key, shape, pieces, low, high):
    gain = 1.0
    for dim, parts in pieces:
        heights = jax.random.uniform(jax.random.fold_in(jax.random.fold_in(own_key, 6), dim), (parts,), jnp.float32, low / len(pieces), high / len(pieces))
        gain = gain * jnp.repeat(jnp.exp(heights), shape[dim] // parts).reshape((-1,) + (1,) * (len(shape) - 1 - dim))
    return gain


def setup_inputs(seed: int = 0) -> dict:
    arg_keys = jax.random.split(jax.random.key(seed), 3)
    right_side = draw_right_side(jax.random.fold_in(arg_keys[2], 71), 0)
    density = jnp.clip(jnp.exp(math.log(4.0) - 2.0794415 * jax.random.uniform(arg_keys[1], (NZ, NX, NY), jnp.float32) ** level_of(arg_keys[1], (NZ, NX, NY), ((0, 2), (1, 16)), -0.2, 0.2)), 0.5, 4.0)
    return dict(right_side=right_side, density=density)


relaxation = 0.8
plane_coupling = 16.0
depth_coupling = 1.0


def apply_operator(field, density_level, coupling):
    diagonal = density_level + 4.0 * coupling + 2.0 * depth_coupling
    padded = jnp.pad(field, ((0, 0), (1, 1), (1, 1)))
    lateral = padded[:, 2:, 1:-1] + padded[:, :-2, 1:-1] + padded[:, 1:-1, 2:] + padded[:, 1:-1, :-2]
    vertical = jnp.roll(field, 1, axis=0) + jnp.roll(field, -1, axis=0)
    return diagonal * field - coupling * lateral - depth_coupling * vertical, diagonal


def relax_once(field, source, density_level, coupling):
    image, diagonal = apply_operator(field, density_level, coupling)
    return field + relaxation * (source - image) / diagonal


def restrict(values):
    rows_z, rows_x, rows_y = values.shape
    return values.reshape(rows_z, rows_x // 2, 2, rows_y // 2, 2).mean(axis=(2, 4))


def prolong(values):
    return jnp.repeat(jnp.repeat(values, 2, axis=1), 2, axis=2)


def vcycle(field, source, density_levels, level_index):
    coupling = plane_coupling / 4.0 ** level_index
    density_level = density_levels[level_index]
    if level_index == LEVELS - 1:
        for sweep_index in range(COARSE_SWEEPS):
            field = relax_once(field, source, density_level, coupling)
        return field
    for sweep_index in range(PRE):
        field = relax_once(field, source, density_level, coupling)
    image, diagonal = apply_operator(field, density_level, coupling)
    coarse_source = restrict(source - image)
    correction = vcycle(jnp.zeros_like(coarse_source), coarse_source, density_levels, level_index + 1)
    field = field + prolong(correction)
    for sweep_index in range(POST):
        field = relax_once(field, source, density_level, coupling)
    return field


def reference(right_side, density):
    density_levels = [density]
    for level_index in range(1, LEVELS):
        density_levels.append(restrict(density_levels[-1]))

    def solve_component(source):
        field = jnp.zeros_like(source)
        for cycle_index in range(CYCLES):
            field = vcycle(field, source, density_levels, 0)
        return field

    return lax.map(solve_component, right_side)
```

```python
import functools
import jax
import jax.numpy as jnp
from jax import lax
from jax.experimental import pallas as pl
from jax.experimental.pallas import tpu as pltpu
from jax.sharding import PartitionSpec as P

LEVELS = 4
CYCLES = 2
relaxation = 0.8
plane_coupling = 16.0
depth_coupling = 1.0
SUB, LANE = 8, 128
COUPLING = [plane_coupling / 4.0**level for level in range(LEVELS)]
HALO = [5, 2, 2, 2]
MESH = pl.DeviceIdType.MESH


def iotas():
    return (
        lax.broadcasted_iota(jnp.int32, (SUB, LANE), 0),
        lax.broadcasted_iota(jnp.int32, (SUB, LANE), 1),
    )


def y_sum(v, k):
    sub, lane = iotas()
    from_low = pltpu.roll(v, k, 2)
    from_high = pltpu.roll(v, LANE - k, 2)
    low_carry = jnp.where(sub == 0, 0.0, pltpu.roll(from_low, 1, 1))
    high_carry = jnp.where(sub == SUB - 1, 0.0, pltpu.roll(from_high, SUB - 1, 1))
    return jnp.where(lane < k, low_carry, from_low) + jnp.where(lane >= LANE - k, high_carry, from_high)


def neighbours(src, row, c, v, level):
    lateral = src[row - 1, c] + src[row + 1, c] + y_sum(v, 1 << level)
    vertical = jnp.concatenate([v[-1:], v[:-1]], 0) + jnp.concatenate([v[1:], v[:1]], 0)
    return COUPLING[level] * lateral + depth_coupling * vertical


def pair_sum(v, level):
    k = 1 << level
    _, lane = iotas()
    low = (lane & k) == 0
    return v + jnp.where(low, pltpu.roll(v, LANE - k, 2), pltpu.roll(v, k, 2))


def pack(planes, p):
    if p == 1:
        return planes
    _, lane = iotas()
    groups = -(-len(planes) // p)
    out = []
    for g in range(groups):
        value = planes[g]
        for j in range(1, p):
            if j * groups + g < len(planes):
                value = jnp.where((lane & (p - 1)) == j, planes[j * groups + g], value)
        out.append(value)
    return out


def unpack(groups, count, p):
    _, lane = iotas()
    out = []
    for index in range(count):
        j, g = divmod(index, len(groups))
        value, bit = groups[g], 1
        while bit < p:
            if j & bit:
                value = jnp.where((lane & bit) != 0, value, pltpu.roll(value, LANE - bit, 1))
            else:
                value = jnp.where((lane & bit) == 0, value, pltpu.roll(value, bit, 1))
            bit *= 2
        out.append(value)
    return out


def kernel(plan, block, out, *scratch):
    nx_dev, nz_dev, comps, nz_own, nz, rows = (
        plan[k] for k in ("gx", "gz", "comps", "nz_own", "nz", "rows"))
    refs = dict(zip(plan["names"], scratch))
    send_sem, recv_sem, local_sem = refs["send"], refs["recv"], refs["local"]
    me, mz = lax.axis_index("gx"), lax.axis_index("gz")
    z0 = mz * nz_own
    counter = [0]

    def there(offset):
        target = me + offset
        return jnp.logical_and(target >= 0, target < nx_dev)

    offsets = (-1, 1, -2, 2)
    barrier = pltpu.get_barrier_semaphore()
    expected = nz_dev - 1
    for step in range(1, nz_dev):
        pl.semaphore_signal(barrier, inc=1, device_id={"gz": lax.rem(mz + step, nz_dev)}, device_id_type=MESH)
    for offset in offsets:
        expected = expected + there(offset).astype(jnp.int32)

        @pl.when(there(offset))
        def _():
            pl.semaphore_signal(barrier, inc=1, device_id={"gx": me + offset}, device_id_type=MESH)

    pl.semaphore_wait(barrier, expected)

    def send(offset, src, dst):
        index = counter[0]
        counter[0] += 1
        copy = pltpu.make_async_remote_copy(
            src_ref=src, dst_ref=dst, send_sem=send_sem.at[index], recv_sem=recv_sem.at[index],
            device_id={"gx": me + offset}, device_id_type=MESH)

        @pl.when(there(offset))
        def _():
            copy.start()

        def finish(received=lambda: None, absent=lambda: None):
            @pl.when(there(offset))
            def _():
                copy.wait_send()

            @pl.when(there(-offset))
            def _():
                copy.wait_recv()
                received()

            @pl.when(jnp.logical_not(there(-offset)))
            def _():
                absent()

        return finish

    def zero_rows(ref, low, high):
        def run():
            for row in range(low, high):
                ref[row] = jnp.zeros(ref.shape[1:], ref.dtype)
        return run

    s0 = refs["s0"]
    h0 = HALO[0]
    own = s0.at[pl.ds(h0, rows[0]), :, pl.ds(z0, nz_own)]
    local = pltpu.make_async_copy(block, own, local_sem)
    local.start()
    gathers = []
    for step in range(1, nz_dev):
        index = counter[0]
        counter[0] += 1
        copy = pltpu.make_async_remote_copy(
            src_ref=block, dst_ref=own, send_sem=send_sem.at[index], recv_sem=recv_sem.at[index],
            device_id={"gz": lax.rem(mz + step, nz_dev)}, device_id_type=MESH)
        copy.start()
        gathers.append(copy)
    local.wait()
    for copy in gathers:
        copy.wait()

    n0 = rows[0]
    near = [
        send(-1, s0.at[h0:h0 + 2], s0.at[h0 + n0:h0 + n0 + 2]),
        send(1, s0.at[h0 + n0 - 2:h0 + n0], s0.at[h0 - 2:h0]),
    ]
    far = [
        send(-1, s0.at[h0 + 2:h0 + 4], s0.at[h0 + n0 + 2:h0 + n0 + 4]),
        send(1, s0.at[h0 + n0 - 4:h0 + n0 - 2], s0.at[h0 - 4:h0 - 2]),
    ]

    def loop(low, high, body):
        lax.fori_loop(low, high, lambda row, carry: (body(row), 0)[1], 0)

    def weights(level, low, high):
        s, w, h, n = refs[f"s{level}"], refs[f"w{level}"], HALO[level], rows[level]

        def body(row):
            place = row - h + me * n
            inside = jnp.logical_and(place >= 0, place < n * nx_dev)
            scale = jnp.where(inside, relaxation, 0.0).astype(jnp.float32)
            w[row] = scale / (s[row, comps] + 4.0 * COUPLING[level] + 2.0 * depth_coupling)

        loop(h + low, h + high, body)

    def first_sweep(level, dst, extra):
        s, w, h, n = refs[f"s{level}"], refs[f"w{level}"], HALO[level], rows[level]

        def body(row):
            weight = w[row]
            for c in range(comps):
                dst[row, c] = weight * s[row, c]

        loop(h - extra, h + n + extra, body)

    def sweep(level, src, dst, extra, last=False):
        s, w, h, n = refs[f"s{level}"], refs[f"w{level}"], HALO[level], rows[level]

        def body(row):
            weight = w[row]
            for c in range(comps):
                v = src[row, c]
                dst[row, c] = (1.0 - relaxation) * v + weight * (s[row, c] + neighbours(src, row, c, v, level))
            if last:
                out[row - h] = dst[row, :, pl.ds(z0, nz_own)]

        loop(h - extra, h + n + extra, body)

    def restrict(level, src, with_density):
        s, h, n = refs[f"s{level}"], HALO[level], rows[level]
        coarse, hc = refs[f"s{level + 1}"], HALO[level + 1]

        def body(index):
            for c in range(comps):
                total = None
                for part in range(2):
                    row = h + 2 * index + part
                    v = src[row, c]
                    diagonal = s[row, comps] + 4.0 * COUPLING[level] + 2.0 * depth_coupling
                    value = s[row, c] - diagonal * v + neighbours(src, row, c, v, level)
                    total = value if total is None else total + value
                coarse[hc + index, c] = 0.25 * pair_sum(total, level)
            if with_density:
                total = s[h + 2 * index, comps] + s[h + 2 * index + 1, comps]
                coarse[hc + index, comps] = 0.25 * pair_sum(total, level)

        loop(0, rows[level + 1], body)

    def halo(level, ref, count, tag):
        p, h, n = 1 << level, HALO[level], rows[level]
        out_buf, in_buf = refs[f"out_{tag}"], refs[f"in_{tag}"]
        for row in range(n):
            planes = [ref[h + row, c, z] for c in range(count) for z in range(nz)]
            for g, value in enumerate(pack(planes, p)):
                out_buf[row, g] = value
        finishes = []
        width = min(n, 2)
        for slot, offset in enumerate(offsets if n == 1 else offsets[:2]):
            first = 0 if offset < 0 else n - width
            finishes.append((send(offset, out_buf.at[first:first + width], in_buf.at[slot]), slot, offset))
        for finish, slot, offset in finishes:
            if n == 1:
                start = h - offset
            else:
                start = h + n if offset < 0 else h - width

            def received(slot=slot, start=start):
                for row in range(width):
                    groups = [in_buf[slot, row, g] for g in range(in_buf.shape[2])]
                    for index, value in enumerate(unpack(groups, count * nz, p)):
                        ref[start + row, index // nz, index % nz] = value

            finish(received, zero_rows(ref, start, start + width))

    def correct(level, field, dst):
        h, n = HALO[level], rows[level]
        hc = HALO[level + 1]
        coarse = refs[f"a{level + 1}"]

        def body(index):
            for part in range(2):
                for c in range(comps):
                    dst[h + 2 * index + part, c] = field[h + 2 * index + part, c] + coarse[hc + index, c]

        loop(0, rows[level + 1], body)

    def coarse_cycle(level, cycle):
        s, a, b = refs[f"s{level}"], refs[f"a{level}"], refs[f"b{level}"]
        h, n = HALO[level], rows[level]
        halo(level, s, comps + (1 if cycle == 0 else 0), f"s{level}_{cycle}")
        if cycle == 0:
            weights(level, -2, n + 2)
        first_sweep(level, a, 2)
        sweep(level, a, b, 1)
        if level == LEVELS - 1:
            sweep(level, b, a, 0)
            return
        restrict(level, b, cycle == 0)
        coarse_cycle(level + 1, cycle)
        correct(level, b, a)
        halo(level, a, comps, f"v{level}_{cycle}")
        sweep(level, a, b, 1)
        sweep(level, b, a, 0)

    a0, b0 = refs["a0"], refs["b0"]
    near[0](absent=zero_rows(s0, h0 + n0, h0 + n0 + 2))
    near[1](absent=zero_rows(s0, h0 - 2, h0))
    weights(0, -2, n0 + 2)
    first_sweep(0, a0, 2)
    for cycle in range(CYCLES):
        if cycle == 0:
            sweep(0, a0, b0, 1)
        restrict(0, b0, cycle == 0)
        coarse_cycle(1, cycle)
        fresh = refs[f"f{cycle}"]
        correct(0, b0, fresh)
        wide = 5 if cycle < CYCLES - 1 else 2
        ends = [
            send(-1, fresh.at[h0:h0 + wide], fresh.at[h0 + n0:h0 + n0 + wide]),
            send(1, fresh.at[h0 + n0 - wide:h0 + n0], fresh.at[h0 - wide:h0]),
        ]
        if cycle == 0:
            far[0](absent=zero_rows(s0, h0 + n0 + 2, h0 + n0 + 4))
            far[1](absent=zero_rows(s0, h0 - 4, h0 - 2))
            weights(0, -4, -2)
            weights(0, n0 + 2, n0 + 4)
        ends[0](absent=zero_rows(fresh, h0 + n0, h0 + n0 + wide))
        ends[1](absent=zero_rows(fresh, h0 - wide, h0))
        if cycle < CYCLES - 1:
            sweep(0, fresh, a0, 4)
            sweep(0, a0, b0, 3)
            sweep(0, b0, a0, 2)
            sweep(0, a0, b0, 1)
        else:
            sweep(0, fresh, a0, 1)
            sweep(0, a0, b0, 0, last=True)


def shards(plan, right_side, density):
    comps, nz_own, n0, ny = right_side.shape
    block = jnp.concatenate([right_side, density[None]], 0)
    block = block.reshape(comps + 1, nz_own, n0, SUB, LANE).transpose(2, 0, 1, 3, 4)
    nz = nz_own * plan["gz"]
    rows = [n0 >> level for level in range(LEVELS)]
    shapes = {}

    def buf(name, *shape):
        shapes[name] = pltpu.VMEM(shape + (SUB, LANE), jnp.float32)

    for level in range(LEVELS):
        total = rows[level] + 2 * HALO[level]
        buf(f"s{level}", total, comps + 1, nz)
        buf(f"w{level}", total, nz)
        buf(f"a{level}", total, comps, nz)
        buf(f"b{level}", total, comps, nz)
    for cycle in range(CYCLES):
        buf(f"f{cycle}", rows[0] + 2 * HALO[0], comps, nz)
        for level in range(1, LEVELS):
            n = rows[level]
            for kind, count in (("s", comps + (cycle == 0)), ("v", comps)):
                if kind == "v" and level == LEVELS - 1:
                    continue
                groups = -(-count * nz // (1 << level))
                buf(f"out_{kind}{level}_{cycle}", n, groups)
                buf(f"in_{kind}{level}_{cycle}", 4 if n == 1 else 2, min(n, 2), groups)
    sems = plan["gz"] - 1 + 4 + CYCLES * (2 + 2 * 2 * (LEVELS - 2) + 4)
    shapes["send"] = pltpu.SemaphoreType.DMA((sems,))
    shapes["recv"] = pltpu.SemaphoreType.DMA((sems,))
    shapes["local"] = pltpu.SemaphoreType.DMA
    plan = dict(plan, comps=comps, nz_own=nz_own, nz=nz, rows=rows, names=list(shapes))
    result = pl.pallas_call(
        functools.partial(kernel, plan),
        out_shape=jax.ShapeDtypeStruct((n0, comps, nz_own, SUB, LANE), jnp.float32),
        in_specs=[pl.BlockSpec(memory_space=pltpu.VMEM)],
        out_specs=pl.BlockSpec(memory_space=pltpu.VMEM),
        scratch_shapes=list(shapes.values()),
        compiler_params=pltpu.CompilerParams(
            collective_id=0, has_side_effects=True, vmem_limit_bytes=60 * 1024 * 1024),
    )(block)
    return result.transpose(1, 2, 0, 3, 4).reshape(comps, nz_own, n0, ny)


def solution(mesh):
    plan = dict(gx=mesh.shape["gx"], gz=mesh.shape["gz"])
    return jax.shard_map(
        functools.partial(shards, plan),
        mesh=mesh,
        in_specs=(P(None, "gz", "gx", None), P("gz", "gx", None)),
        out_specs=P(None, "gz", "gx", None),
        check_vma=False,
    )
```

```python
import functools
import jax
import jax.numpy as jnp
from jax import lax
from jax.experimental import pallas as pl
from jax.experimental.pallas import tpu as pltpu
from jax.sharding import PartitionSpec as P

LEVELS = 4
CYCLES = 2
relaxation = 0.8
plane_coupling = 16.0
depth_coupling = 1.0
SUB, LANE = 8, 128
COUPLING = [plane_coupling / 4.0**level for level in range(LEVELS)]
HALO = [5, 2, 2, 2]
SKEW = 0
MESH = pl.DeviceIdType.MESH


def iotas():
    return (
        lax.broadcasted_iota(jnp.int32, (SUB, LANE), 0),
        lax.broadcasted_iota(jnp.int32, (SUB, LANE), 1),
    )


def y_sum(v, k):
    shape = v.shape
    v = v.reshape((-1, SUB, LANE))
    sub, lane = iotas()
    from_low = pltpu.roll(v, k, 2)
    from_high = pltpu.roll(v, LANE - k, 2)
    low_carry = jnp.where(sub == 0, 0.0, pltpu.roll(from_low, 1, 1))
    high_carry = jnp.where(sub == SUB - 1, 0.0, pltpu.roll(from_high, SUB - 1, 1))
    total = jnp.where(lane < k, low_carry, from_low) + jnp.where(lane >= LANE - k, high_carry, from_high)
    return total.reshape(shape)


def neighbours(strip, level):
    v = strip[1:-1]
    lateral = strip[:-2] + strip[2:] + y_sum(v, 1 << level)
    vertical = jnp.concatenate([v[:, -1:], v[:, :-1]], 1) + jnp.concatenate([v[:, 1:], v[:, :1]], 1)
    return COUPLING[level] * lateral + depth_coupling * vertical


def pair_sum(v, level):
    k = 1 << level
    _, lane = iotas()
    low = (lane & k) == 0
    return v + jnp.where(low, pltpu.roll(v, LANE - k, 2), pltpu.roll(v, k, 2))


def pack(planes, p):
    if p == 1:
        return planes
    _, lane = iotas()
    groups = -(-len(planes) // p)
    out = []
    for g in range(groups):
        value = planes[g]
        for j in range(1, p):
            if j * groups + g < len(planes):
                value = jnp.where((lane & (p - 1)) == j, planes[j * groups + g], value)
        out.append(value)
    return out


def unpack(groups, count, p):
    _, lane = iotas()
    out = []
    for index in range(count):
        j, g = divmod(index, len(groups))
        value, bit = groups[g], 1
        while bit < p:
            if j & bit:
                value = jnp.where((lane & bit) != 0, value, pltpu.roll(value, LANE - bit, 1))
            else:
                value = jnp.where((lane & bit) == 0, value, pltpu.roll(value, bit, 1))
            bit *= 2
        out.append(value)
    return out


def kernel(plan, block, out, *scratch):
    nx_dev, nz_dev, comps, nz_own, nz, rows = (
        plan[k] for k in ("gx", "gz", "comps", "nz_own", "nz", "rows"))
    refs = dict(zip(plan["names"], scratch))
    send_sem, recv_sem, local_sem = refs["send"], refs["recv"], refs["local"]
    me, mz = lax.axis_index("gx"), lax.axis_index("gz")
    z0 = mz * nz_own
    counter = [0]
    dens = comps

    def there(offset):
        target = me + offset
        return jnp.logical_and(target >= 0, target < nx_dev)

    offsets = (-1, 1, -2, 2)
    barrier = pltpu.get_barrier_semaphore()
    expected = nz_dev - 1
    for step in range(1, nz_dev):
        pl.semaphore_signal(barrier, inc=1, device_id={"gz": lax.rem(mz + step, nz_dev)}, device_id_type=MESH)
    for offset in offsets:
        expected = expected + there(offset).astype(jnp.int32)

        @pl.when(there(offset))
        def _():
            pl.semaphore_signal(barrier, inc=1, device_id={"gx": me + offset}, device_id_type=MESH)

    pl.semaphore_wait(barrier, expected)

    def send(offset, src, dst):
        index = counter[0]
        counter[0] += 1
        copy = pltpu.make_async_remote_copy(
            src_ref=src, dst_ref=dst, send_sem=send_sem.at[index], recv_sem=recv_sem.at[index],
            device_id={"gx": me + offset}, device_id_type=MESH)

        @pl.when(there(offset))
        def _():
            copy.start()

        def finish(received=lambda: None, absent=lambda: None):
            @pl.when(there(-offset))
            def _():
                copy.wait_recv()
                received()

            @pl.when(jnp.logical_not(there(-offset)))
            def _():
                absent()

            @pl.when(there(offset))
            def _():
                copy.wait_send()

        return finish

    def zero_rows(ref, low, high):
        def run():
            for row in range(low, high):
                ref[row] = jnp.zeros(ref.shape[1:], ref.dtype)
        return run

    def loop(low, high, body):
        step = 2 if (high - low) % 2 == 0 else 1
        count = (high - low) // step
        if count <= 2 or step == 1:
            for index in range(count):
                body(low + index * step, step)
        else:
            lax.fori_loop(0, count, lambda i, carry: (body(low + i * step, step), 0)[1], 0)

    def weights(level, low, high):
        s, w, h, n = refs[f"s{level}"].at[dens], refs[f"w{level}"], HALO[level], rows[level]
        for row in range(h + low, h + high):
            place = row - h + me * n
            inside = jnp.logical_and(place >= 0, place < n * nx_dev)
            scale = jnp.where(inside, relaxation, 0.0).astype(jnp.float32)
            w[row] = scale / (s[row] + 4.0 * COUPLING[level] + 2.0 * depth_coupling)

    def first_sweep(level, c, dst, extra):
        s, w, h, n = refs[f"s{level}"].at[c], refs[f"w{level}"], HALO[level], rows[level]

        def body(row, m):
            here = pl.ds(row, m)
            dst[here] = w[here] * s[here]

        loop(h - extra, h + n + extra, body)

    def sweep(level, c, src, dst, extra, last=False):
        s, w, h, n = refs[f"s{level}"].at[c], refs[f"w{level}"], HALO[level], rows[level]

        def body(row, m):
            here = pl.ds(row, m)
            strip = src[pl.ds(row - 1, m + 2)]
            dst[here] = (1.0 - relaxation) * strip[1:-1] + w[here] * (s[here] + neighbours(strip, level))
            if last:
                out[c, pl.ds(row - h, m)] = dst[here, pl.ds(z0, nz_own)]

        loop(h - extra, h + n + extra, body)

    def restrict(level, c, src):
        s, d, h = refs[f"s{level}"].at[c], refs[f"s{level}"].at[dens], HALO[level]
        coarse, hc = refs[f"s{level + 1}"].at[c], HALO[level + 1]

        def body(row, m):
            here = pl.ds(row, m)
            strip = src[pl.ds(row - 1, m + 2)]
            diagonal = d[here] + 4.0 * COUPLING[level] + 2.0 * depth_coupling
            value = s[here] - diagonal * strip[1:-1] + neighbours(strip, level)
            place = hc + (row - h) // 2
            coarse[place] = 0.25 * pair_sum(value[0] + value[1], level)

        loop(h, h + rows[level], body)

    def restrict_density(level):
        fine, h = refs[f"s{level}"].at[dens], HALO[level]
        coarse, hc = refs[f"s{level + 1}"].at[dens], HALO[level + 1]
        for index in range(rows[level + 1]):
            coarse[hc + index] = 0.25 * pair_sum(fine[h + 2 * index] + fine[h + 2 * index + 1], level)

    def halo(level, ref, tag, c):
        p, h, n = 1 << level, HALO[level], rows[level]
        out_buf, in_buf = refs[f"out_{tag}"].at[c], refs[f"in_{tag}"].at[c]
        for row in range(n):
            for g, value in enumerate(pack([ref[h + row, z] for z in range(nz)], p)):
                out_buf[row, g] = value
        finishes = []
        width = min(n, 2)
        for slot, offset in enumerate(offsets if n == 1 else offsets[:2]):
            first = 0 if offset < 0 else n - width
            finishes.append((send(offset, out_buf.at[first:first + width], in_buf.at[slot]), slot, offset))

        def finish_all():
            for finish, slot, offset in finishes:
                if n == 1:
                    start = h - offset
                else:
                    start = h + n if offset < 0 else h - width

                def received(slot=slot, start=start):
                    for row in range(width):
                        groups = [in_buf[slot, row, g] for g in range(in_buf.shape[2])]
                        for z, value in enumerate(unpack(groups, nz, p)):
                            ref[start + row, z] = value

                finish(received, zero_rows(ref, start, start + width))

        return finish_all

    def correct(level, c, field, dst):
        h, n, hc = HALO[level], rows[level], HALO[level + 1]
        coarse = refs[f"a{level + 1}"].at[c]
        for index in range(rows[level + 1]):
            value = coarse[hc + index]
            for part in range(2):
                row = h + 2 * index + part
                dst[row] = field[row] + value

    h0, n0 = HALO[0], rows[0]
    s0 = refs["s0"]

    def gather(c):
        own = s0.at[c, pl.ds(h0, n0), pl.ds(z0, nz_own)]
        copies = [pltpu.make_async_copy(block.at[c], own, local_sem.at[c])]
        for step in range(1, nz_dev):
            index = counter[0]
            counter[0] += 1
            copies.append(pltpu.make_async_remote_copy(
                src_ref=block.at[c], dst_ref=own, send_sem=send_sem.at[index], recv_sem=recv_sem.at[index],
                device_id={"gz": lax.rem(mz + step, nz_dev)}, device_id_type=MESH))
        for copy in reversed(copies):
            copy.start()

        def finish():
            for copy in copies:
                copy.wait()

        return finish

    def ends(ref, skip, width):
        low, high = h0 + n0 + skip, h0 - skip
        left = send(-1, ref.at[h0 + skip:h0 + skip + width], ref.at[low:low + width])
        right = send(1, ref.at[h0 + n0 - skip - width:h0 + n0 - skip], ref.at[high - width:high])

        def finish():
            left(absent=zero_rows(ref, low, low + width))
            right(absent=zero_rows(ref, high - width, high))

        return finish

    density = {}

    def coarse_cycle(level, c, cycle):
        s, a, b = (refs[f"{kind}{level}"].at[c] for kind in "sab")
        h, n = HALO[level], rows[level]
        finish = halo(level, s, f"s{level}_{cycle}", c)
        yield
        if cycle == 0 and c == 0:
            density.pop(level)()
            weights(level, -2, n + 2)
        finish()
        first_sweep(level, c, a, 2)
        sweep(level, c, a, b, 1)
        if level == LEVELS - 1:
            sweep(level, c, b, a, 0)
            return
        restrict(level, c, b)
        yield from coarse_cycle(level + 1, c, cycle)
        correct(level, c, b, a)
        finish = halo(level, a, f"v{level}_{cycle}", c)
        yield
        finish()
        sweep(level, c, a, b, 1)
        sweep(level, c, b, a, 0)

    gathers = {c: gather(c) for c in [dens] + list(range(comps))}

    def component(c):
        a0, b0 = refs["a0"].at[c], refs["b0"].at[c]
        if c == 0:
            gathers[dens]()
            density["near"] = ends(s0.at[dens], 0, 2)
        gathers[c]()
        finish = ends(s0.at[c], 0, 2)
        if c == 0:
            for level in range(LEVELS - 1):
                restrict_density(level)
        yield
        if c == 0:
            density.pop("near")()
            weights(0, -2, n0 + 2)
            for level in range(1, LEVELS):
                density[level] = halo(level, refs[f"s{level}"].at[dens], f"s{level}_0", dens)
            density["far"] = ends(s0.at[dens], 2, 2)
        finish()
        far = ends(s0.at[c], 2, 2)
        first_sweep(0, c, a0, 2)
        sweep(0, c, a0, b0, 1)
        for cycle in range(CYCLES):
            restrict(0, c, b0)
            yield from coarse_cycle(1, c, cycle)
            fresh = refs[f"f{cycle}"].at[c]
            correct(0, c, b0, fresh)
            finish = ends(fresh, 0, 5 if cycle < CYCLES - 1 else 2)
            yield
            if cycle == 0:
                if c == 0:
                    density.pop("far")()
                    weights(0, -4, -2)
                    weights(0, n0 + 2, n0 + 4)
                far()
            finish()
            if cycle < CYCLES - 1:
                sweep(0, c, fresh, a0, 4)
                sweep(0, c, a0, b0, 3)
                sweep(0, c, b0, a0, 2)
                sweep(0, c, a0, b0, 1)
            else:
                sweep(0, c, fresh, a0, 1)
                sweep(0, c, a0, b0, 0, last=True)

    waiting = [component(c) for c in range(comps)]
    turn = 0
    while any(part is not None for part in waiting):
        for c in range(comps):
            if waiting[c] is not None and turn >= c * SKEW:
                try:
                    next(waiting[c])
                except StopIteration:
                    waiting[c] = None
        turn += 1
    assert counter[0] == send_sem.shape[0]


def shards(plan, right_side, density):
    comps, nz_own, n0, ny = right_side.shape
    block = jnp.concatenate([right_side, density[None]], 0)
    block = block.reshape(comps + 1, nz_own, n0, SUB, LANE).transpose(0, 2, 1, 3, 4)
    nz = nz_own * plan["gz"]
    rows = [n0 >> level for level in range(LEVELS)]
    shapes = {}

    def buf(name, *shape):
        shapes[name] = pltpu.VMEM(shape + (SUB, LANE), jnp.float32)

    for level in range(LEVELS):
        total = rows[level] + 2 * HALO[level]
        buf(f"s{level}", comps + 1, total, nz)
        buf(f"w{level}", total, nz)
        buf(f"a{level}", comps, total, nz)
        buf(f"b{level}", comps, total, nz)
    sems = (comps + 1) * (plan["gz"] - 1)
    for cycle in range(CYCLES):
        buf(f"f{cycle}", comps, rows[0] + 2 * HALO[0], nz)
        sems += comps * 2
        for level in range(1, LEVELS):
            n = rows[level]
            for kind, count in (("s", comps + (cycle == 0)), ("v", comps)):
                if kind == "v" and level == LEVELS - 1:
                    continue
                groups = -(-nz // (1 << level))
                buf(f"out_{kind}{level}_{cycle}", count, n, groups)
                buf(f"in_{kind}{level}_{cycle}", count, 4 if n == 1 else 2, min(n, 2), groups)
                sems += count * (4 if n == 1 else 2)
    sems += (comps + 1) * 4
    shapes["send"] = pltpu.SemaphoreType.DMA((sems,))
    shapes["recv"] = pltpu.SemaphoreType.DMA((sems,))
    shapes["local"] = pltpu.SemaphoreType.DMA((comps + 1,))
    plan = dict(plan, comps=comps, nz_own=nz_own, nz=nz, rows=rows, names=list(shapes))
    result = pl.pallas_call(
        functools.partial(kernel, plan),
        out_shape=jax.ShapeDtypeStruct((comps, n0, nz_own, SUB, LANE), jnp.float32),
        in_specs=[pl.BlockSpec(memory_space=pltpu.VMEM)],
        out_specs=pl.BlockSpec(memory_space=pltpu.VMEM),
        scratch_shapes=list(shapes.values()),
        compiler_params=pltpu.CompilerParams(
            collective_id=0, has_side_effects=True, vmem_limit_bytes=60 * 1024 * 1024),
    )(block)
    return result.transpose(0, 2, 1, 3, 4).reshape(comps, nz_own, n0, ny)


def solution(mesh):
    plan = dict(gx=mesh.shape["gx"], gz=mesh.shape["gz"])
    return jax.shard_map(
        functools.partial(shards, plan),
        mesh=mesh,
        in_specs=(P(None, "gz", "gx", None), P("gz", "gx", None)),
        out_specs=P(None, "gz", "gx", None),
        check_vma=False,
    )
```

```python
import functools
import jax
import jax.numpy as jnp
from jax import lax
from jax.experimental import pallas as pl
from jax.experimental.pallas import tpu as pltpu
from jax.sharding import PartitionSpec as P

LEVELS = 4
CYCLES = 2
relaxation = 0.8
plane_coupling = 16.0
depth_coupling = 1.0
SUB, LANE = 8, 128
COUPLING = [plane_coupling / 4.0**level for level in range(LEVELS)]
MERGED = False
BEYOND = [[5, 3, 3, 3] if MERGED else [0, 0, 1, 2], [0, 0, 1, 2]]
REACH = [
    [6 if MERGED else 2] + [BEYOND[cycle][level] + (3 if level < LEVELS - 1 else 2) for level in range(1, LEVELS)]
    for cycle in range(CYCLES)
]
HALO = [6 if MERGED else 5] + REACH[0][1:]
SKEW = 0
MESH = pl.DeviceIdType.MESH


def iotas():
    return (
        lax.broadcasted_iota(jnp.int32, (SUB, LANE), 0),
        lax.broadcasted_iota(jnp.int32, (SUB, LANE), 1),
    )


def y_sum(v, k):
    shape = v.shape
    v = v.reshape((-1, SUB, LANE))
    sub, lane = iotas()
    from_low = pltpu.roll(v, k, 2)
    from_high = pltpu.roll(v, LANE - k, 2)
    low_carry = jnp.where(sub == 0, 0.0, pltpu.roll(from_low, 1, 1))
    high_carry = jnp.where(sub == SUB - 1, 0.0, pltpu.roll(from_high, SUB - 1, 1))
    total = jnp.where(lane < k, low_carry, from_low) + jnp.where(lane >= LANE - k, high_carry, from_high)
    return total.reshape(shape)


def neighbours(strip, level):
    v = strip[1:-1]
    lateral = strip[:-2] + strip[2:] + y_sum(v, 1 << level)
    vertical = jnp.concatenate([v[:, -1:], v[:, :-1]], 1) + jnp.concatenate([v[:, 1:], v[:, :1]], 1)
    return COUPLING[level] * lateral + vertical


def pair_sum(v, level):
    k = 1 << level
    _, lane = iotas()
    low = (lane & k) == 0
    return v + jnp.where(low, pltpu.roll(v, LANE - k, 2), pltpu.roll(v, k, 2))


def pack(planes, p):
    if p == 1:
        return planes
    _, lane = iotas()
    groups = -(-len(planes) // p)
    out = []
    for g in range(groups):
        value = planes[g]
        for j in range(1, p):
            if j * groups + g < len(planes):
                value = jnp.where((lane & (p - 1)) == j, planes[j * groups + g], value)
        out.append(value)
    return out


def unpack(groups, count, p):
    _, lane = iotas()
    out = []
    for index in range(count):
        j, g = divmod(index, len(groups))
        value, bit = groups[g], 1
        while bit < p:
            if j & bit:
                value = jnp.where((lane & bit) != 0, value, pltpu.roll(value, LANE - bit, 1))
            else:
                value = jnp.where((lane & bit) == 0, value, pltpu.roll(value, bit, 1))
            bit *= 2
        out.append(value)
    return out


def messages(n, reach):
    return [
        (sign * far, min(n, reach - (far - 1) * n))
        for far in range(1, -(-reach // n) + 1)
        for sign in (-1, 1)
    ]


def kernel(plan, block, out, *scratch):
    nx_dev, nz_dev, comps, nz_own, nz, rows = (
        plan[k] for k in ("gx", "gz", "comps", "nz_own", "nz", "rows"))
    refs = dict(zip(plan["names"], scratch))
    send_sem, recv_sem, local_sem = refs["send"], refs["recv"], refs["local"]
    me, mz = lax.axis_index("gx"), lax.axis_index("gz")
    z0 = mz * nz_own
    counter = [0]
    dens = comps

    def there(offset):
        target = me + offset
        return jnp.logical_and(target >= 0, target < nx_dev)

    offsets = [sign * far for far in range(1, plan["far"] + 1) for sign in (-1, 1)]
    barrier = pltpu.get_barrier_semaphore()
    expected = nz_dev - 1
    for step in range(1, nz_dev):
        pl.semaphore_signal(barrier, inc=1, device_id={"gz": lax.rem(mz + step, nz_dev)}, device_id_type=MESH)
    for offset in offsets:
        expected = expected + there(offset).astype(jnp.int32)

        @pl.when(there(offset))
        def _():
            pl.semaphore_signal(barrier, inc=1, device_id={"gx": me + offset}, device_id_type=MESH)

    pl.semaphore_wait(barrier, expected)

    def send(offset, src, dst):
        index = counter[0]
        counter[0] += 1
        copy = pltpu.make_async_remote_copy(
            src_ref=src, dst_ref=dst, send_sem=send_sem.at[index], recv_sem=recv_sem.at[index],
            device_id={"gx": me + offset}, device_id_type=MESH)

        @pl.when(there(offset))
        def _():
            copy.start()

        def finish(received=lambda: None, absent=lambda: None):
            @pl.when(there(-offset))
            def _():
                copy.wait_recv()
                received()

            @pl.when(jnp.logical_not(there(-offset)))
            def _():
                absent()

            @pl.when(there(offset))
            def _():
                copy.wait_send()

        return finish

    def zero_rows(ref, low, high):
        def run():
            for row in range(low, high):
                ref[row] = jnp.zeros(ref.shape[1:], ref.dtype)
        return run

    def loop(low, high, body, step=None):
        if step is None:
            step = max(m for m in range(1, max(1, 30 // nz) + 1) if (high - low) % m == 0)
        count = (high - low) // step
        if count <= 3:
            for index in range(count):
                body(low + index * step, step)
        else:
            lax.fori_loop(0, count, lambda i, carry: (body(low + i * step, step), 0)[1], 0)

    def weights(level, low, high):
        s, w, h, n = refs[f"s{level}"].at[dens], refs[f"w{level}"], HALO[level], rows[level]
        for row in range(h + low, h + high):
            place = row - h + me * n
            inside = jnp.logical_and(place >= 0, place < n * nx_dev)
            scale = jnp.where(inside, relaxation, 0.0).astype(jnp.float32)
            w[row] = scale / (s[row] + 4.0 * COUPLING[level] + 2.0 * depth_coupling)

    def first_sweep(level, c, dst, extra):
        s, w, h, n = refs[f"s{level}"].at[c], refs[f"w{level}"], HALO[level], rows[level]

        def body(row, m):
            here = pl.ds(row, m)
            dst[here] = w[here] * s[here]

        loop(h - extra, h + n + extra, body)

    def sweep(level, c, src, dst, extra, last=False):
        s, w, h, n = refs[f"s{level}"].at[c], refs[f"w{level}"], HALO[level], rows[level]

        def body(row, m):
            here = pl.ds(row, m)
            strip = src[pl.ds(row - 1, m + 2)]
            dst[here] = (1.0 - relaxation) * strip[1:-1] + w[here] * (s[here] + neighbours(strip, level))
            if last:
                out[c, pl.ds(row - h, m)] = dst[here, pl.ds(z0, nz_own)]

        loop(h - extra, h + n + extra, body)

    def restrict(level, c, src):
        s, d, h = refs[f"s{level}"].at[c], refs[f"s{level}"].at[dens], HALO[level]
        coarse, hc = refs[f"s{level + 1}"].at[c], HALO[level + 1]

        def body(row, m):
            here = pl.ds(row, m)
            strip = src[pl.ds(row - 1, m + 2)]
            diagonal = d[here] + 4.0 * COUPLING[level] + 2.0 * depth_coupling
            value = s[here] - diagonal * strip[1:-1] + neighbours(strip, level)
            place = hc + (row - h) // 2
            coarse[place] = 0.25 * pair_sum(value[0] + value[1], level)

        loop(h, h + rows[level], body, 2)

    def restrict_density(level):
        fine, h = refs[f"s{level}"].at[dens], HALO[level]
        coarse, hc = refs[f"s{level + 1}"].at[dens], HALO[level + 1]
        for index in range(rows[level + 1]):
            coarse[hc + index] = 0.25 * pair_sum(fine[h + 2 * index] + fine[h + 2 * index + 1], level)

    def halo(level, ref, tag, c, reach):
        p, h, n = 1 << level, HALO[level], rows[level]
        out_buf, in_buf = refs[f"out_{tag}"].at[c], refs[f"in_{tag}"].at[c]
        for row in range(n):
            for g, value in enumerate(pack([ref[h + row, z] for z in range(nz)], p)):
                out_buf[row, g] = value
        finishes = []
        for slot, (offset, width) in enumerate(messages(n, reach)):
            first = 0 if offset < 0 else n - width
            start = h - (offset - 1) * n - width if offset > 0 else h - offset * n
            target = in_buf.at[slot, 0:width]
            finishes.append((send(offset, out_buf.at[first:first + width], target), slot, start, width))

        def finish_all():
            for finish, slot, start, width in finishes:

                def received(slot=slot, start=start, width=width):
                    for row in range(width):
                        groups = [in_buf[slot, row, g] for g in range(in_buf.shape[2])]
                        for z, value in enumerate(unpack(groups, nz, p)):
                            ref[start + row, z] = value

                finish(received, zero_rows(ref, start, start + width))

        return finish_all

    def correct(level, c, field, dst, extra):
        h, n, hc = HALO[level], rows[level], HALO[level + 1]
        coarse = refs[f"a{level + 1}"]
        for index in range(-((extra + 1) // 2), (n + extra + 1) // 2):
            value = coarse[hc + index]
            for row in range(max(2 * index, -extra), min(2 * index + 2, n + extra)):
                dst[h + row] = field[h + row] + value

    h0, n0 = HALO[0], rows[0]
    s0 = refs["s0"]

    def gather(c):
        own = s0.at[c, pl.ds(h0, n0), pl.ds(z0, nz_own)]
        copies = [pltpu.make_async_copy(block.at[c], own, local_sem.at[c])]
        for step in range(1, nz_dev):
            index = counter[0]
            counter[0] += 1
            copies.append(pltpu.make_async_remote_copy(
                src_ref=block.at[c], dst_ref=own, send_sem=send_sem.at[index], recv_sem=recv_sem.at[index],
                device_id={"gz": lax.rem(mz + step, nz_dev)}, device_id_type=MESH))
        for copy in reversed(copies):
            copy.start()

        def finish():
            for copy in copies:
                copy.wait()

        return finish

    def ends(ref, skip, width):
        low, high = h0 + n0 + skip, h0 - skip
        left = send(-1, ref.at[h0 + skip:h0 + skip + width], ref.at[low:low + width])
        right = send(1, ref.at[h0 + n0 - skip - width:h0 + n0 - skip], ref.at[high - width:high])

        def finish():
            left(absent=zero_rows(ref, low, low + width))
            right(absent=zero_rows(ref, high - width, high))

        return finish

    density = {}

    def coarse_cycle(level, c, cycle):
        s, a, b = refs[f"s{level}"].at[c], refs[f"a{level}"], refs[f"b{level}"].at[c]
        n, reach, beyond = rows[level], REACH[cycle][level], BEYOND[cycle][level]
        finish = halo(level, s, f"s{level}_{cycle}", c, reach)
        yield
        if cycle == 0 and c == 0:
            density.pop(level)()
            weights(level, -reach, n + reach)
        finish()
        first_sweep(level, c, a, reach)
        sweep(level, c, a, b, reach - 1)
        if level == LEVELS - 1:
            sweep(level, c, b, a, reach - 2)
            return
        restrict(level, c, b)
        yield from coarse_cycle(level + 1, c, cycle)
        correct(level, c, b, a, beyond + 2)
        sweep(level, c, a, b, beyond + 1)
        sweep(level, c, b, a, beyond)

    gathers = {c: gather(c) for c in [dens] + list(range(comps))}

    def component(c):
        a0, b0 = refs["a0"], refs["b0"].at[c]
        reach = REACH[0][0]
        if c == 0:
            gathers[dens]()
            density["near"] = ends(s0.at[dens], 0, reach)
        gathers[c]()
        finish = ends(s0.at[c], 0, reach)
        if c == 0:
            for level in range(LEVELS - 1):
                restrict_density(level)
        yield
        if c == 0:
            density.pop("near")()
            weights(0, -reach, n0 + reach)
            for level in range(1, LEVELS):
                density[level] = halo(level, refs[f"s{level}"].at[dens], f"s{level}_0", dens, REACH[0][level])
            if not MERGED:
                density["far"] = ends(s0.at[dens], 2, 2)
        finish()
        if not MERGED:
            far = ends(s0.at[c], 2, 2)
        first_sweep(0, c, a0, reach)
        sweep(0, c, a0, b0, reach - 1)
        for cycle in range(CYCLES):
            restrict(0, c, b0)
            yield from coarse_cycle(1, c, cycle)
            fresh = refs[f"f{cycle}"].at[c]
            merged = MERGED and cycle == 0
            correct(0, c, b0, fresh, 5 if merged else 0)
            if not merged:
                finish = ends(fresh, 0, 5 if cycle < CYCLES - 1 else 2)
                yield
                if cycle == 0:
                    if c == 0:
                        density.pop("far")()
                        weights(0, -4, -2)
                        weights(0, n0 + 2, n0 + 4)
                    far()
                finish()
            if cycle < CYCLES - 1:
                sweep(0, c, fresh, a0, 4)
                sweep(0, c, a0, b0, 3)
                sweep(0, c, b0, a0, 2)
                sweep(0, c, a0, b0, 1)
            else:
                sweep(0, c, fresh, a0, 1)
                sweep(0, c, a0, b0, 0, last=True)

    waiting = [component(c) for c in range(comps)]
    turn = 0
    while any(part is not None for part in waiting):
        for c in range(comps):
            if waiting[c] is not None and turn >= c * SKEW:
                try:
                    next(waiting[c])
                except StopIteration:
                    waiting[c] = None
        turn += 1
    assert counter[0] == send_sem.shape[0]


def shards(plan, right_side, density):
    comps, nz_own, n0, ny = right_side.shape
    block = jnp.concatenate([right_side, density[None]], 0)
    block = block.reshape(comps + 1, nz_own, n0, SUB, LANE).transpose(0, 2, 1, 3, 4)
    nz = nz_own * plan["gz"]
    rows = [n0 >> level for level in range(LEVELS)]
    shapes = {}

    def buf(name, *shape):
        shapes[name] = pltpu.VMEM(shape + (SUB, LANE), jnp.float32)

    for level in range(LEVELS):
        total = rows[level] + 2 * HALO[level]
        buf(f"s{level}", comps + 1, total, nz)
        buf(f"w{level}", total, nz)
        buf(f"a{level}", total, nz)
        buf(f"b{level}", comps, total, nz)
    sems = (comps + 1) * (plan["gz"] - 1)
    far = 1
    for cycle in range(CYCLES):
        buf(f"f{cycle}", comps, rows[0] + 2 * HALO[0], nz)
        for level in range(1, LEVELS):
            n, count = rows[level], comps + (cycle == 0)
            groups = -(-nz // (1 << level))
            sent = messages(n, REACH[cycle][level])
            buf(f"out_s{level}_{cycle}", count, n, groups)
            buf(f"in_s{level}_{cycle}", count, len(sent), sent[0][1], groups)
            sems += count * len(sent)
            far = max(far, sent[-1][0])
    sems += (comps + 1) * 2 + (comps * 2 if MERGED else (comps + 1) * 2 + comps * 4)
    shapes["send"] = pltpu.SemaphoreType.DMA((sems,))
    shapes["recv"] = pltpu.SemaphoreType.DMA((sems,))
    shapes["local"] = pltpu.SemaphoreType.DMA((comps + 1,))
    plan = dict(plan, far=far, comps=comps, nz_own=nz_own, nz=nz, rows=rows, names=list(shapes))
    result = pl.pallas_call(
        functools.partial(kernel, plan),
        out_shape=jax.ShapeDtypeStruct((comps, n0, nz_own, SUB, LANE), jnp.float32),
        in_specs=[pl.BlockSpec(memory_space=pltpu.VMEM)],
        out_specs=pl.BlockSpec(memory_space=pltpu.VMEM),
        scratch_shapes=list(shapes.values()),
        compiler_params=pltpu.CompilerParams(
            collective_id=0, has_side_effects=True, vmem_limit_bytes=60 * 1024 * 1024),
    )(block)
    return result.transpose(0, 2, 1, 3, 4).reshape(comps, nz_own, n0, ny)


def solution(mesh):
    plan = dict(gx=mesh.shape["gx"], gz=mesh.shape["gz"])
    return jax.shard_map(
        functools.partial(shards, plan),
        mesh=mesh,
        in_specs=(P(None, "gz", "gx", None), P("gz", "gx", None)),
        out_specs=P(None, "gz", "gx", None),
        check_vma=False,
    )
```

```python
import functools
import jax
import jax.numpy as jnp
from jax import lax
from jax.experimental import pallas as pl
from jax.experimental.pallas import tpu as pltpu
from jax.sharding import PartitionSpec as P

LEVELS = 4
CYCLES = 2
relaxation = 0.8
plane_coupling = 16.0
depth_coupling = 1.0
SUB, LANE = 8, 128
COUPLING = [plane_coupling / 4.0**level for level in range(LEVELS)]
MERGED = False
BEYOND = [[5, 3, 3, 3] if MERGED else [0, 0, 1, 2], [0, 0, 1, 2]]
REACH = [
    [6 if MERGED else 2] + [BEYOND[cycle][level] + (3 if level < LEVELS - 1 else 2) for level in range(1, LEVELS)]
    for cycle in range(CYCLES)
]
HALO = [6 if MERGED else 5] + REACH[0][1:]
SKEW = 0
MESH = pl.DeviceIdType.MESH


def iotas():
    return (
        lax.broadcasted_iota(jnp.int32, (SUB, LANE), 0),
        lax.broadcasted_iota(jnp.int32, (SUB, LANE), 1),
    )


def y_sum(v, k):
    shape = v.shape
    v = v.reshape((-1, SUB, LANE))
    sub, lane = iotas()
    from_low = pltpu.roll(v, k, 2)
    from_high = pltpu.roll(v, LANE - k, 2)
    low_carry = jnp.where(sub == 0, 0.0, pltpu.roll(from_low, 1, 1))
    high_carry = jnp.where(sub == SUB - 1, 0.0, pltpu.roll(from_high, SUB - 1, 1))
    total = jnp.where(lane < k, low_carry, from_low) + jnp.where(lane >= LANE - k, high_carry, from_high)
    return total.reshape(shape)


def turn_classes(v, level, classes, step):
    if level == 0:
        return v
    shape = v.shape
    v = v.reshape((-1, SUB, LANE))
    _, lane = iotas()
    place = lane & ((1 << level) - 1)
    if step > 0:
        v = jnp.where(place < classes - 1, pltpu.roll(v, LANE - 1, 2), pltpu.roll(v, classes - 1, 2))
    else:
        v = jnp.where(place > 0, pltpu.roll(v, 1, 2), pltpu.roll(v, LANE - (classes - 1), 2))
    return v.reshape(shape)


def neighbours(strip, level, classes):
    v = strip[1:-1]
    lateral = strip[:-2] + strip[2:] + y_sum(v, 1 << level)
    before = turn_classes(v[:, -1:], level, classes, -1)
    after = turn_classes(v[:, :1], level, classes, 1)
    if v.shape[1] > 1:
        before = jnp.concatenate([before, v[:, :-1]], 1)
        after = jnp.concatenate([v[:, 1:], after], 1)
    vertical = before + after
    return COUPLING[level] * lateral + vertical


def pair_sum(v, level):
    k = 1 << level
    _, lane = iotas()
    low = (lane & k) == 0
    return v + jnp.where(low, pltpu.roll(v, LANE - k, 2), pltpu.roll(v, k, 2))


def pack(planes, p):
    if p == 1:
        return planes
    _, lane = iotas()
    groups = -(-len(planes) // p)
    out = []
    for g in range(groups):
        value = planes[g]
        for j in range(1, p):
            if j * groups + g < len(planes):
                value = jnp.where((lane & (p - 1)) == j, planes[j * groups + g], value)
        out.append(value)
    return out


def unpack(groups, count, p):
    _, lane = iotas()
    out = []
    for index in range(count):
        j, g = divmod(index, len(groups))
        value, bit = groups[g], 1
        while bit < p:
            if j & bit:
                value = jnp.where((lane & bit) != 0, value, pltpu.roll(value, LANE - bit, 1))
            else:
                value = jnp.where((lane & bit) == 0, value, pltpu.roll(value, bit, 1))
            bit *= 2
        out.append(value)
    return out


def messages(n, reach):
    return [
        (sign * far, min(n, reach - (far - 1) * n))
        for far in range(1, -(-reach // n) + 1)
        for sign in (-1, 1)
    ]


def kernel(plan, block, out, *scratch):
    nx_dev, nz_dev, comps, nz_own, nz, rows = (
        plan[k] for k in ("gx", "gz", "comps", "nz_own", "nz", "rows"))
    refs = dict(zip(plan["names"], scratch))
    send_sem, recv_sem, local_sem = refs["send"], refs["recv"], refs["local"]
    me, mz = lax.axis_index("gx"), lax.axis_index("gz")
    z0 = mz * nz_own
    counter = [0]
    dens = comps
    groups = plan["groups"]
    classes = [nz // g for g in groups]

    def repack(value, level, target):
        planes = unpack([value[g] for g in range(value.shape[0])], nz, 1 << level)
        return jnp.stack(pack(planes, 1 << target))

    def there(offset):
        target = me + offset
        return jnp.logical_and(target >= 0, target < nx_dev)

    offsets = [sign * far for far in range(1, plan["far"] + 1) for sign in (-1, 1)]
    barrier = pltpu.get_barrier_semaphore()
    expected = nz_dev - 1
    for step in range(1, nz_dev):
        pl.semaphore_signal(barrier, inc=1, device_id={"gz": lax.rem(mz + step, nz_dev)}, device_id_type=MESH)
    for offset in offsets:
        expected = expected + there(offset).astype(jnp.int32)

        @pl.when(there(offset))
        def _():
            pl.semaphore_signal(barrier, inc=1, device_id={"gx": me + offset}, device_id_type=MESH)

    pl.semaphore_wait(barrier, expected)

    def send(offset, src, dst):
        index = counter[0]
        counter[0] += 1
        copy = pltpu.make_async_remote_copy(
            src_ref=src, dst_ref=dst, send_sem=send_sem.at[index], recv_sem=recv_sem.at[index],
            device_id={"gx": me + offset}, device_id_type=MESH)

        @pl.when(there(offset))
        def _():
            copy.start()

        def finish(received=lambda: None, absent=lambda: None):
            @pl.when(there(-offset))
            def _():
                copy.wait_recv()
                received()

            @pl.when(jnp.logical_not(there(-offset)))
            def _():
                absent()

            @pl.when(there(offset))
            def _():
                copy.wait_send()

        return finish

    def zero_rows(ref, low, high):
        def run():
            for row in range(low, high):
                ref[row] = jnp.zeros(ref.shape[1:], ref.dtype)
        return run

    def loop(low, high, body, step=None, width=nz):
        if step is None:
            step = max(m for m in range(1, max(1, 30 // width) + 1) if (high - low) % m == 0)
        count = (high - low) // step
        if count <= 3:
            for index in range(count):
                body(low + index * step, step)
        else:
            lax.fori_loop(0, count, lambda i, carry: (body(low + i * step, step), 0)[1], 0)

    def weights(level, low, high):
        s, w, h, n = refs[f"s{level}"].at[dens], refs[f"w{level}"], HALO[level], rows[level]
        for row in range(h + low, h + high):
            place = row - h + me * n
            inside = jnp.logical_and(place >= 0, place < n * nx_dev)
            scale = jnp.where(inside, relaxation, 0.0).astype(jnp.float32)
            w[row] = scale / (s[row] + 4.0 * COUPLING[level] + 2.0 * depth_coupling)

    def first_sweep(level, c, dst, extra):
        s, w, h, n = refs[f"s{level}"].at[c], refs[f"w{level}"], HALO[level], rows[level]

        def body(row, m):
            here = pl.ds(row, m)
            dst[here] = w[here] * s[here]

        loop(h - extra, h + n + extra, body, None, groups[level])

    def sweep(level, c, src, dst, extra, last=False):
        s, w, h, n = refs[f"s{level}"].at[c], refs[f"w{level}"], HALO[level], rows[level]

        def body(row, m):
            here = pl.ds(row, m)
            strip = src[pl.ds(row - 1, m + 2)]
            dst[here] = (1.0 - relaxation) * strip[1:-1] + w[here] * (s[here] + neighbours(strip, level, classes[level]))
            if last:
                out[c, pl.ds(row - h, m)] = dst[here, pl.ds(z0, nz_own)]

        loop(h - extra, h + n + extra, body, None, groups[level])

    def restrict(level, c, src):
        s, d, h = refs[f"s{level}"].at[c], refs[f"s{level}"].at[dens], HALO[level]
        coarse, hc = refs[f"s{level + 1}"].at[c], HALO[level + 1]

        def body(row, m):
            here = pl.ds(row, m)
            strip = src[pl.ds(row - 1, m + 2)]
            diagonal = d[here] + 4.0 * COUPLING[level] + 2.0 * depth_coupling
            value = s[here] - diagonal * strip[1:-1] + neighbours(strip, level, classes[level])
            place = hc + (row - h) // 2
            coarse[place] = repack(0.25 * pair_sum(value[0] + value[1], level), level, level + 1)

        loop(h, h + rows[level], body, 2)

    def restrict_density(level):
        fine, h = refs[f"s{level}"].at[dens], HALO[level]
        coarse, hc = refs[f"s{level + 1}"].at[dens], HALO[level + 1]
        for index in range(rows[level + 1]):
            total = fine[h + 2 * index] + fine[h + 2 * index + 1]
            coarse[hc + index] = repack(0.25 * pair_sum(total, level), level, level + 1)

    def halo(level, ref, tag, c, reach):
        h, n = HALO[level], rows[level]
        in_buf = refs[f"in_{tag}"].at[c]
        finishes = []
        for slot, (offset, width) in enumerate(messages(n, reach)):
            first = h if offset < 0 else h + n - width
            start = h - (offset - 1) * n - width if offset > 0 else h - offset * n
            target = in_buf.at[slot, 0:width]
            finishes.append((send(offset, ref.at[first:first + width], target), slot, start, width))

        def finish_all():
            for finish, slot, start, width in finishes:

                def received(slot=slot, start=start, width=width):
                    for row in range(width):
                        ref[start + row] = in_buf[slot, row]

                finish(received, zero_rows(ref, start, start + width))

        return finish_all

    def correct(level, c, field, dst, extra):
        h, n, hc = HALO[level], rows[level], HALO[level + 1]
        coarse = refs[f"a{level + 1}"]
        for index in range(-((extra + 1) // 2), (n + extra + 1) // 2):
            value = repack(coarse[hc + index], level + 1, level)
            for row in range(max(2 * index, -extra), min(2 * index + 2, n + extra)):
                dst[h + row] = field[h + row] + value

    h0, n0 = HALO[0], rows[0]
    s0 = refs["s0"]

    def gather(c):
        own = s0.at[c, pl.ds(h0, n0), pl.ds(z0, nz_own)]
        copies = [pltpu.make_async_copy(block.at[c], own, local_sem.at[c])]
        for step in range(1, nz_dev):
            index = counter[0]
            counter[0] += 1
            copies.append(pltpu.make_async_remote_copy(
                src_ref=block.at[c], dst_ref=own, send_sem=send_sem.at[index], recv_sem=recv_sem.at[index],
                device_id={"gz": lax.rem(mz + step, nz_dev)}, device_id_type=MESH))
        for copy in reversed(copies):
            copy.start()

        def finish():
            for copy in copies:
                copy.wait()

        return finish

    def ends(ref, skip, width):
        low, high = h0 + n0 + skip, h0 - skip
        left = send(-1, ref.at[h0 + skip:h0 + skip + width], ref.at[low:low + width])
        right = send(1, ref.at[h0 + n0 - skip - width:h0 + n0 - skip], ref.at[high - width:high])

        def finish():
            left(absent=zero_rows(ref, low, low + width))
            right(absent=zero_rows(ref, high - width, high))

        return finish

    density = {}

    def coarse_cycle(level, c, cycle):
        s, a, b = refs[f"s{level}"].at[c], refs[f"a{level}"], refs[f"b{level}"].at[c]
        n, reach, beyond = rows[level], REACH[cycle][level], BEYOND[cycle][level]
        finish = halo(level, s, f"s{level}_{cycle}", c, reach)
        yield
        if cycle == 0 and c == 0:
            density.pop(level)()
            weights(level, -reach, n + reach)
        finish()
        first_sweep(level, c, a, reach)
        sweep(level, c, a, b, reach - 1)
        if level == LEVELS - 1:
            sweep(level, c, b, a, reach - 2)
            return
        restrict(level, c, b)
        yield from coarse_cycle(level + 1, c, cycle)
        correct(level, c, b, a, beyond + 2)
        sweep(level, c, a, b, beyond + 1)
        sweep(level, c, b, a, beyond)

    gathers = {c: gather(c) for c in [dens] + list(range(comps))}

    def component(c):
        a0, b0 = refs["a0"], refs["b0"].at[c]
        reach = REACH[0][0]
        if c == 0:
            gathers[dens]()
            density["near"] = ends(s0.at[dens], 0, reach)
        gathers[c]()
        finish = ends(s0.at[c], 0, reach)
        if c == 0:
            for level in range(LEVELS - 1):
                restrict_density(level)
        yield
        if c == 0:
            density.pop("near")()
            weights(0, -reach, n0 + reach)
            for level in range(1, LEVELS):
                density[level] = halo(level, refs[f"s{level}"].at[dens], f"s{level}_0", dens, REACH[0][level])
            if not MERGED:
                density["far"] = ends(s0.at[dens], 2, 2)
        finish()
        if not MERGED:
            far = ends(s0.at[c], 2, 2)
        first_sweep(0, c, a0, reach)
        sweep(0, c, a0, b0, reach - 1)
        for cycle in range(CYCLES):
            restrict(0, c, b0)
            yield from coarse_cycle(1, c, cycle)
            fresh = refs[f"f{cycle}"].at[c]
            merged = MERGED and cycle == 0
            correct(0, c, b0, fresh, 5 if merged else 0)
            if not merged:
                finish = ends(fresh, 0, 5 if cycle < CYCLES - 1 else 2)
                yield
                if cycle == 0:
                    if c == 0:
                        density.pop("far")()
                        weights(0, -4, -2)
                        weights(0, n0 + 2, n0 + 4)
                    far()
                finish()
            if cycle < CYCLES - 1:
                sweep(0, c, fresh, a0, 4)
                sweep(0, c, a0, b0, 3)
                sweep(0, c, b0, a0, 2)
                sweep(0, c, a0, b0, 1)
            else:
                sweep(0, c, fresh, a0, 1)
                sweep(0, c, a0, b0, 0, last=True)

    waiting = [component(c) for c in range(comps)]
    turn = 0
    while any(part is not None for part in waiting):
        for c in range(comps):
            if waiting[c] is not None and turn >= c * SKEW:
                try:
                    next(waiting[c])
                except StopIteration:
                    waiting[c] = None
        turn += 1
    assert counter[0] == send_sem.shape[0]


def shards(plan, right_side, density):
    comps, nz_own, n0, ny = right_side.shape
    block = jnp.concatenate([right_side, density[None]], 0)
    block = block.reshape(comps + 1, nz_own, n0, SUB, LANE).transpose(0, 2, 1, 3, 4)
    nz = nz_own * plan["gz"]
    rows = [n0 >> level for level in range(LEVELS)]
    groups = [-(-nz // (1 << level)) for level in range(LEVELS)]
    assert all(nz % g == 0 for g in groups)
    shapes = {}

    def buf(name, *shape):
        shapes[name] = pltpu.VMEM(shape + (SUB, LANE), jnp.float32)

    for level in range(LEVELS):
        total = rows[level] + 2 * HALO[level]
        buf(f"s{level}", comps + 1, total, groups[level])
        buf(f"w{level}", total, groups[level])
        buf(f"a{level}", total, groups[level])
        buf(f"b{level}", comps, total, groups[level])
    sems = (comps + 1) * (plan["gz"] - 1)
    far = 1
    for cycle in range(CYCLES):
        buf(f"f{cycle}", comps, rows[0] + 2 * HALO[0], nz)
        for level in range(1, LEVELS):
            n, count = rows[level], comps + (cycle == 0)
            sent = messages(n, REACH[cycle][level])
            buf(f"in_s{level}_{cycle}", count, len(sent), sent[0][1], groups[level])
            sems += count * len(sent)
            far = max(far, sent[-1][0])
    sems += (comps + 1) * 2 + (comps * 2 if MERGED else (comps + 1) * 2 + comps * 4)
    shapes["send"] = pltpu.SemaphoreType.DMA((sems,))
    shapes["recv"] = pltpu.SemaphoreType.DMA((sems,))
    shapes["local"] = pltpu.SemaphoreType.DMA((comps + 1,))
    plan = dict(plan, far=far, groups=groups, comps=comps, nz_own=nz_own, nz=nz, rows=rows, names=list(shapes))
    result = pl.pallas_call(
        functools.partial(kernel, plan),
        out_shape=jax.ShapeDtypeStruct((comps, n0, nz_own, SUB, LANE), jnp.float32),
        in_specs=[pl.BlockSpec(memory_space=pltpu.VMEM)],
        out_specs=pl.BlockSpec(memory_space=pltpu.VMEM),
        scratch_shapes=list(shapes.values()),
        compiler_params=pltpu.CompilerParams(
            collective_id=0, has_side_effects=True, vmem_limit_bytes=60 * 1024 * 1024),
    )(block)
    return result.transpose(0, 2, 1, 3, 4).reshape(comps, nz_own, n0, ny)


def solution(mesh):
    plan = dict(gx=mesh.shape["gx"], gz=mesh.shape["gz"])
    return jax.shard_map(
        functools.partial(shards, plan),
        mesh=mesh,
        in_specs=(P(None, "gz", "gx", None), P("gz", "gx", None)),
        out_specs=P(None, "gz", "gx", None),
        check_vma=False,
    )
```
